768 devices in a mesh: rep: 96 (over z, x, core), fsdp: 8 (over y).
Axes of the slice: x: 4, y: 8, z: 12, core: 2. Of those that a mesh axis runs over, the one named last changes fastest.
Arguments:
- grads: bfloat16 [96, 8, 128, 6144], P('rep', 'fsdp'), may hold values from -4 to 4
- momentum: float32 [96, 128, 6144], P('rep', None, 'fsdp'), may hold values from -6 to 6
- indices: int32 [96, 2, 96, 32], P(None, None, 'fsdp'), may hold values from 0 to 4095, as said below
Outputs:
- new_momentum: float32 [96, 128, 6144], P('rep', None, 'fsdp')
- update: float32 [128, 6144], P(None, 'fsdp')
The draws below stay inside these ranges and needn't reach their ends.
Inputs may be any that keep to these rules, and one draw needn't show every extreme that they name: `indices`: within each block the 32 positions are distinct, and position k lies in [k * 64 * 2, (k + 1) * 64 * 2). The positions are fixed in advance and known to every replica (they stand in for DeMo's top-k choice, which is not part of this step).
All inputs are finite; a program needn't handle non-finite values.
Results may differ from the reference program's by a relative error of at most 0.0003.
Values sent between devices are 32-bit elements; how exact they have to be, the bound alone decides.
A program may use at most 32 MiB of HBM per device.

```python
import jax
import jax.numpy as jnp
from jax import lax

D = 6144
SPAN = 64
KEEP = 32
ROWS = 128
N_REP = 96
N_FSDP = 8


def draw_indices(key, part):
    key = jax.random.fold_in(key, 7)
    spacing = SPAN * SPAN // KEEP
    offsets = jax.random.randint(key, (N_REP, ROWS // SPAN, D // SPAN, KEEP), 0, spacing)
    starts = jnp.arange(KEEP, dtype=jnp.int32) * spacing
    positions = offsets.astype(jnp.int32) + starts
    positions = positions.at[0, 0, 0, 0].set(0)
    positions = positions.at[0, 0, 0, KEEP - 1].set(SPAN * SPAN - 1)
    return positions.astype(jnp.int32)


def with_spikes(array, key, source, target, parts, factor):
    def block_of(position):
        return (jnp.arange(array.shape[position]) // (array.shape[position] // parts)).reshape((-1,) + (1,) * (array.ndim - 1 - position))

    first = jax.random.permutation(key, parts)[block_of(target)]
    second = (block_of(target) + parts // 2) % parts
    return jnp.where((block_of(source) == first) | (block_of(source) == second), factor * array, array)


def steps_of(own_key, dims, pieces, least, top_value):
    level, own = 1.0, jax.random.fold_in(own_key, 6)
    for dim, blocks in pieces:
        draws = jnp.exp(jax.random.uniform(jax.random.fold_in(own, dim), (blocks,), jnp.float32, least / len(pieces), top_value / len(pieces)))
        level = level * jnp.repeat(draws, dims[dim] // blocks).reshape([-1 if axis == dim else 1 for axis in range(len(dims))])
    return level


def gaussian(own_key, shape, scale, most, split=(), held_as=jnp.bfloat16):
    array = scale * jax.random.normal(own_key, shape, jnp.float32)
    if split:
        array = array * steps_of(own_key, shape, split, -0.22, 0.18)
    return jnp.clip(array, -most, most).astype(held_as)


def heavy_noise(own_key, dims, scale, limit, split, heavy, held_as=jnp.bfloat16):
    result = scale * jax.random.normal(own_key, dims, jnp.float32)
    if split:
        result = result * steps_of(own_key, dims, split, -0.22, 0.18)
    return jnp.clip(with_spikes(result, jax.random.fold_in(own_key, 3), *heavy), -limit, limit).astype(held_as)


def setup_inputs(seed: int = 0) -> dict:
    keys = jax.random.split(jax.random.key(seed), 4)
    return {
        "grads": heavy_noise(keys[0], (N_REP, N_FSDP, ROWS, D), 0.5, 4.0, ((0, 96), (1, 8)), (1, 3, 8, 2.0)),
        "momentum": gaussian(keys[1], (N_REP, ROWS, D), 1.0, 6.0, ((0, 96), (2, 8)), jnp.float32),
        "indices": draw_indices(jax.random.fold_in(keys[3], 71), 0),
    }


decay_rate = 0.999

def cosine_table():
    freq = jnp.arange(SPAN, dtype=jnp.float32)[:, None]
    sample = jnp.arange(SPAN, dtype=jnp.float32)[None, :]
    table = jnp.cos(jnp.pi * (2.0 * sample + 1.0) * freq / (2.0 * SPAN))
    scales = jnp.where(freq == 0, jnp.sqrt(1.0 / SPAN), jnp.sqrt(2.0 / SPAN))
    return table * scales

def to_blocks(matrix):
    height, width = matrix.shape
    return matrix.reshape(height // SPAN, SPAN, width // SPAN, SPAN).transpose(0, 2, 1, 3)

def from_blocks(blocks):
    bands, groups = (blocks.shape[0], blocks.shape[1])
    return blocks.transpose(0, 2, 1, 3).reshape(bands * SPAN, groups * SPAN)

def forward_transform(matrix, table):
    blocks = to_blocks(matrix)
    spectra = jnp.einsum('ij,acjk,lk->acil', table, blocks, table, precision=lax.Precision.HIGHEST)
    return spectra.reshape(spectra.shape[0], spectra.shape[1], SPAN * SPAN)

def inverse_transform(flat, table):
    spectra = flat.reshape(flat.shape[0], flat.shape[1], SPAN, SPAN)
    blocks = jnp.einsum('ij,acil,lk->acjk', table, spectra, table, precision=lax.Precision.HIGHEST)
    return from_blocks(blocks)

def place(total, values, positions):
    band_ids = jnp.arange(total.shape[0], dtype=jnp.int32)[:, None, None]
    group_ids = jnp.arange(total.shape[1], dtype=jnp.int32)[None, :, None]
    return total.at[band_ids, group_ids, positions].add(values)

def reference(grads, momentum, indices):
    table = cosine_table()

    def one_replica(running, inputs):
        partial_grads, old_momentum, positions = inputs
        gradient = lax.optimization_barrier(jnp.sum(partial_grads.astype(jnp.float32), axis=0))
        fresh = decay_rate * old_momentum + gradient
        spectra = forward_transform(fresh, table)
        kept = jnp.take_along_axis(spectra, positions, axis=2)
        own = place(jnp.zeros_like(spectra), kept, positions)
        remaining = fresh - inverse_transform(own, table)
        return (running + own, remaining)
    start_total = jnp.zeros((indices.shape[1], indices.shape[2], SPAN * SPAN), momentum.dtype)
    total, new_momentum = lax.scan(one_replica, start_total, (grads, momentum, indices))
    update = inverse_transform(total, table)
    return (new_momentum, update)
```

```python
import functools

import jax
import jax.numpy as jnp
import numpy as np
from jax import lax
from jax.experimental import pallas as pl
from jax.experimental.pallas import tpu as pltpu
from jax.sharding import PartitionSpec as P

SPAN = 64
KEEP = 32
LANES = 128
SPACING = SPAN * SPAN // KEEP
CROSS = 8
DECAY = 0.999
MESH = pl.DeviceIdType.MESH


def tables():
    freq = np.arange(SPAN)[:, None]
    sample = np.arange(SPAN)[None, :]
    c = np.cos(np.pi * (2.0 * sample + 1.0) * freq / (2.0 * SPAN))
    c = c * np.where(freq == 0, np.sqrt(1.0 / SPAN), np.sqrt(2.0 / SPAN))
    pair = np.kron(np.eye(2), c)
    halves = [np.kron(np.eye(4), c[i1::2].T) for i1 in range(2)]
    rows_forward = np.concatenate(halves, axis=1)
    halves = [np.tile(np.kron(np.eye(2), c[i1::2].T), (1, 2)) for i1 in range(2)]
    rows_inverse = np.concatenate(halves, axis=1)
    return [t.astype(np.float32) for t in (pair, rows_forward, rows_inverse)]


def split_table(table, axis):
    high = table.astype(jnp.bfloat16)
    low = (table - high.astype(jnp.float32)).astype(jnp.bfloat16)
    return jnp.concatenate([high, high, low], axis=axis)


def split_value(value, axis):
    high = value.astype(jnp.bfloat16)
    low = (value - high.astype(jnp.float32)).astype(jnp.bfloat16)
    return jnp.concatenate([high, low, high], axis=axis)


def dot_nn(a, b):
    return lax.dot_general(a, b, (((1,), (0,)), ((), ())), preferred_element_type=jnp.float32)


def dot_nt(a, b):
    return lax.dot_general(a, b, (((1,), (1,)), ((), ())), preferred_element_type=jnp.float32)


def kernel(
    n_rep, n_ring, pieces, schedule,
    grads_hbm, momentum_hbm, indices_hbm, pair_hbm, rows_forward_hbm, rows_inverse_hbm,
    remaining_hbm, update_hbm,
    grads, momentum, indices, pair, rows_forward, rows_inverse, pair_f, rows_f, rows_i, pair_i,
    first, partial, offsets, fresh, own, kept_all, remaining, update,
    load_sem, chunk_sem, send_sem, recv_sem, z_send, z_recv, x_send, x_recv, out_sem,
):
    width = pieces * LANES
    depth = n_rep // CROSS
    half = SPAN
    rep = lax.axis_index("rep")
    me = lax.axis_index("fsdp")
    z = rep // CROSS
    cross = rep % CROSS
    ring = [lax.rem(me + 1, n_ring), lax.rem(me + n_ring - 1, n_ring)]
    z_peers = [lax.rem(z + d, depth) * CROSS + cross for d in range(1, depth)]
    x_peers = [z * CROSS + lax.rem(cross + d, CROSS) for d in range(1, CROSS)]

    distances = [4, 3, -3, 2, -2, 1, -1, 0]
    chunk_loads = {}
    for slot, distance in enumerate(distances):
        start = pl.multiple_of(lax.rem(me + distance + n_ring, n_ring) * width, LANES)
        columns = pl.ds(start, width)
        chunk_loads[distance] = pltpu.make_async_copy(
            grads_hbm.at[:, columns], grads.at[slot], chunk_sem.at[slot]
        )
        chunk_loads[distance].start()
    loads = [
        pltpu.make_async_copy(source, target, load_sem.at[slot])
        for slot, (source, target) in enumerate(
            [
                (indices_hbm, indices), (pair_hbm, pair), (rows_forward_hbm, rows_forward),
                (rows_inverse_hbm, rows_inverse), (momentum_hbm, momentum),
            ]
        )
    ]
    for load in loads:
        load.start()

    barrier = pltpu.get_barrier_semaphore()
    for neighbour in ring:
        pl.semaphore_signal(barrier, inc=1, device_id=(rep, neighbour), device_id_type=MESH)
    for peer in z_peers + x_peers:
        pl.semaphore_signal(barrier, inc=1, device_id=(peer, me), device_id_type=MESH)

    def own_part(distance, piece, rows=slice(None)):
        slot = distances.index(distance)
        return grads[slot, rows, piece * LANES : (piece + 1) * LANES].astype(jnp.float32)

    def hop(way, step, piece):
        if step == 1:
            rows = pl.ds(0, half) if way == 0 else pl.ds(half, half)
            source = first.at[piece, rows]
            target = partial.at[way, 0, piece, rows]
        else:
            source = partial.at[way, step - 2, piece]
            target = partial.at[way, step - 1, piece]
        return pltpu.make_async_remote_copy(
            src_ref=source,
            dst_ref=target,
            send_sem=send_sem.at[way, step - 1, piece],
            recv_sem=recv_sem.at[way, step - 1, piece],
            device_id=(rep, ring[way]),
            device_id_type=MESH,
        )

    chunk_loads[4].wait()
    for piece in range(pieces):
        first[piece] = own_part(4, piece)
    pl.semaphore_wait(barrier, 2 + len(z_peers) + len(x_peers))

    waited = {4}

    def need(distance):
        if distance not in waited:
            chunk_loads[distance].wait()
            waited.add(distance)

    def send_first(piece):
        for way in range(2):
            hop(way, 1, piece).start()
        need(3)
        need(-3)
        partial[0, 0, piece, half:] = own_part(3, piece, slice(half, None))
        partial[1, 0, piece, :half] = own_part(-3, piece, slice(0, half))

    def send_on(step, piece):
        for way in range(2):
            distance = (5 - step) * (1 if way == 0 else -1)
            need(distance)
            hop(way, step - 1, piece).wait_recv()
            if step == 2:
                rows = slice(0, half) if way == 0 else slice(half, None)
            else:
                rows = slice(None)
            partial[way, step - 2, piece, rows] += own_part(distance, piece, rows)
            hop(way, step, piece).start()

    offset_axis = lax.broadcasted_iota(jnp.int32, (LANES, LANES), 0)
    low_lanes = lax.broadcasted_iota(jnp.int32, (SPAN, 2 * LANES), 1) % LANES < SPAN

    def prepare(piece):
        if piece == 0:
            for load in loads:
                load.wait()
            pair_f[...] = split_table(pair[...], 1)
            rows_f[...] = split_table(rows_forward[...], 0)
            rows_i[...] = split_table(rows_inverse[...], 1)
            pair_i[...] = split_table(pair[...], 0)
        rows = [indices[a, 2 * piece + c] for c in range(2) for a in range(2)]
        positions = jnp.concatenate(rows, axis=0)
        offsets[piece, :n_rep] = jnp.transpose(positions & (SPACING - 1))

    def inverse(spectra):
        wide = jnp.concatenate([spectra[:SPAN], spectra[SPAN:]], axis=1)
        stacked = jnp.concatenate(
            [jnp.where(low_lanes, wide, 0.0), jnp.where(low_lanes, 0.0, wide)], axis=0
        )
        half_way = dot_nt(rows_i[...], split_value(stacked, 1))
        return dot_nn(split_value(half_way, 1), pair_i[...])

    def gather_z(piece, peer):
        row = kept_all.at[piece, cross, z]
        return pltpu.make_async_remote_copy(
            src_ref=row,
            dst_ref=row,
            send_sem=z_send.at[piece],
            recv_sem=z_recv.at[piece],
            device_id=(peer, me),
            device_id_type=MESH,
        )

    def gather_x(piece, peer):
        rows = kept_all.at[piece, cross]
        return pltpu.make_async_remote_copy(
            src_ref=rows,
            dst_ref=rows,
            send_sem=x_send.at[piece],
            recv_sem=x_recv.at[piece],
            device_id=(peer, me),
            device_id_type=MESH,
        )

    def wait_z(piece, sem):
        rows = kept_all.at[piece, 0, pl.ds(0, depth - 1)]
        pltpu.make_async_copy(rows, rows, sem.at[piece]).wait()

    def wait_x(piece, sem):
        rows = kept_all.at[piece, pl.ds(0, CROSS - 1)]
        pltpu.make_async_copy(rows, rows, sem.at[piece]).wait()

    def finish(piece):
        need(0)
        for way in range(2):
            hop(way, 4, piece).wait_recv()
        columns = slice(piece * LANES, (piece + 1) * LANES)
        gradient = own_part(0, piece) + partial[0, 3, piece] + partial[1, 3, piece]
        value = DECAY * momentum[:, columns] + gradient
        fresh[piece] = value
        step = dot_nt(pair_f[...], split_value(value, 1))
        step = jnp.concatenate([step[:SPAN], step[SPAN:]], axis=1)
        step = dot_nn(split_value(step, 1), rows_f[...])
        spectra = jnp.concatenate([step[:, :LANES], step[:, LANES:]], axis=0)
        chosen = jnp.where(offset_axis == offsets[piece, pl.ds(rep, 1)], spectra, 0.0)
        kept_all[piece, cross, z] = jnp.sum(chosen, axis=0, keepdims=True)
        for peer in z_peers:
            gather_z(piece, peer).start()
        own[piece] = chosen

    def subtract(piece):
        columns = slice(piece * LANES, (piece + 1) * LANES)
        remaining[:, columns] = fresh[piece] - inverse(own[piece])

    def pass_on(piece):
        wait_z(piece, z_recv)
        for peer in x_peers:
            gather_x(piece, peer).start()

    def place(piece):
        wait_x(piece, x_recv)

        def add_rows(row, total):
            base = pl.multiple_of(row * CROSS, CROSS)
            for member in range(CROSS):
                position = offsets[piece, pl.ds(base, CROSS)][member : member + 1]
                value = kept_all[piece, member, row]
                total = total + jnp.where(offset_axis == position, value, 0.0)
            return total

        total = lax.fori_loop(0, depth, add_rows, jnp.zeros((LANES, LANES), jnp.float32))
        columns = slice(piece * LANES, (piece + 1) * LANES)
        update[:, columns] = inverse(total)

    stages = {
        "first": send_first, "prepare": prepare, "finish": finish, "subtract": subtract,
        "pass": pass_on, "place": place,
    }
    for stage, piece in schedule:
        if isinstance(stage, int):
            send_on(stage, piece)
        else:
            stages[stage](piece)

    outs = [
        pltpu.make_async_copy(remaining, remaining_hbm, out_sem.at[0]),
        pltpu.make_async_copy(update, update_hbm, out_sem.at[1]),
    ]
    for out in outs:
        out.start()
    for piece in range(pieces):
        for way in range(2):
            for step in range(1, 5):
                hop(way, step, piece).wait_send()
        wait_z(piece, z_send)
        wait_x(piece, x_send)
    for out in outs:
        out.wait()


def order():
    return (
        [("first", p) for p in (0, 1, 2)]
        + [("prepare", p) for p in range(6)]
        + [(s, p) for s in (2, 3, 4) for p in (0, 1, 2)]
        + [("first", p) for p in (3, 4, 5)]
        + [
            ("finish", 0), (2, 3), ("finish", 1), (2, 4), ("pass", 0), ("finish", 2), (2, 5),
            ("pass", 1), ("subtract", 0), (3, 3), ("pass", 2), ("place", 0), (3, 4), ("subtract", 1), ("place", 1),
            (3, 5), ("subtract", 2), (4, 3), ("place", 2), (4, 4), (4, 5),
            ("finish", 3), ("subtract", 3), ("finish", 4), ("pass", 3), ("subtract", 4), ("finish", 5), ("pass", 4),
            ("place", 3), ("pass", 5), ("subtract", 5), ("place", 4), ("place", 5),
        ]
    )


def solution(mesh):
    n_rep, n_ring = mesh.shape["rep"], mesh.shape["fsdp"]
    consts = tables()

    def shards(grads, momentum, indices):
        rows, total_width = grads.shape[2:]
        width = momentum.shape[2]
        pieces = width // LANES
        positions = jnp.transpose(indices, (1, 2, 3, 0))
        grads2, momentum2 = grads.reshape(rows, total_width), momentum.reshape(rows, width)
        f32, bf16 = jnp.float32, jnp.bfloat16
        tile = (LANES, LANES)
        dma = pltpu.SemaphoreType.DMA
        remaining, update = pl.pallas_call(
            functools.partial(kernel, n_rep, n_ring, pieces, order()),
            out_shape=[jax.ShapeDtypeStruct((rows, width), f32)] * 2,
            in_specs=[pl.BlockSpec(memory_space=pl.ANY)] * 6,
            out_specs=[pl.BlockSpec(memory_space=pl.ANY)] * 2,
            scratch_shapes=[
                pltpu.VMEM((n_ring, rows, width), bf16),
                pltpu.VMEM((rows, width), f32),
                pltpu.VMEM(positions.shape, jnp.int32),
                *[pltpu.VMEM(c.shape, f32) for c in consts],
                pltpu.VMEM((LANES, 3 * LANES), bf16),
                pltpu.VMEM((6 * LANES, 2 * LANES), bf16),
                pltpu.VMEM((LANES, 6 * LANES), bf16),
                pltpu.VMEM((3 * LANES, LANES), bf16),
                pltpu.VMEM((pieces, *tile), f32),
                pltpu.VMEM((2, 4, pieces, *tile), f32),
                pltpu.VMEM((pieces, *tile), jnp.int32),
                pltpu.VMEM((pieces, *tile), f32),
                pltpu.VMEM((pieces, *tile), f32),
                pltpu.VMEM((pieces, CROSS, n_rep // CROSS, 1, LANES), f32),
                pltpu.VMEM((rows, width), f32),
                pltpu.VMEM((rows, width), f32),
                dma((5,)),
                dma((n_ring,)),
                dma((2, 4, pieces)),
                dma((2, 4, pieces)),
                dma((pieces,)),
                dma((pieces,)),
                dma((pieces,)),
                dma((pieces,)),
                dma((2,)),
            ],
            compiler_params=pltpu.CompilerParams(
                collective_id=0, has_side_effects=True, vmem_limit_bytes=60 * 2**20
            ),
        )(grads2, momentum2, positions, *[jnp.asarray(c) for c in consts])
        return remaining[None], update

    in_specs = (P("rep", "fsdp", None, None), P("rep", None, "fsdp"), P(None, None, "fsdp", None))
    out_specs = (P("rep", None, "fsdp"), P(None, "fsdp"))
    return jax.shard_map(shards, mesh=mesh, in_specs=in_specs, out_specs=out_specs, check_vma=False)
```

```python
import functools

import jax
import jax.numpy as jnp
import numpy as np
from jax import lax
from jax.experimental import pallas as pl
from jax.experimental.pallas import tpu as pltpu
from jax.sharding import PartitionSpec as P

SPAN = 64
KEEP = 32
LANES = 128
SPACING = SPAN * SPAN // KEEP
CORES = 2
CROSS = 8
DECAY = 0.999
MESH = pl.DeviceIdType.MESH


def tables():
    freq = np.arange(SPAN)[:, None]
    sample = np.arange(SPAN)[None, :]
    c = np.cos(np.pi * (2.0 * sample + 1.0) * freq / (2.0 * SPAN))
    c = c * np.where(freq == 0, np.sqrt(1.0 / SPAN), np.sqrt(2.0 / SPAN))
    pair = np.kron(np.eye(2), c)
    rows = np.concatenate([np.kron(np.eye(2), c[i1::2].T) for i1 in range(2)], axis=1)
    return [t.astype(np.float32) for t in (pair, rows)]


def halves(value):
    high = value.astype(jnp.bfloat16)
    return high, (value - high.astype(jnp.float32)).astype(jnp.bfloat16)


def split_table(table, axis):
    high, low = halves(table)
    return jnp.concatenate([high, high, low], axis=axis)


def split_value(value, axis):
    high, low = halves(value)
    return jnp.concatenate([high, low, high], axis=axis)


def dot_nn(a, b):
    return lax.dot_general(a, b, (((1,), (0,)), ((), ())), preferred_element_type=jnp.float32)


def dot_nt(a, b):
    return lax.dot_general(a, b, (((1,), (1,)), ((), ())), preferred_element_type=jnp.float32)


def kernel(
    n_rep, n_ring, pieces, schedule,
    grads_hbm, momentum_hbm, indices_hbm, pair_hbm, rows_hbm,
    remaining, update,
    grads, momentum, indices, pair, rows, pair_b, pair_f, rows_f, rows_i, pair_i,
    first, partial, offsets, chosen_at, spectra, kept_part, kept_in, kept_own, kept_all,
    load_sem, chunk_sem, send_sem, recv_sem, index_sem, part_sem, z_send, z_recv, x_send, x_recv, update_send, update_recv,
):
    width = pieces * LANES
    depth = n_rep // CROSS
    half = SPAN
    group = pieces // CORES
    rep = lax.axis_index("rep")
    me = lax.axis_index("fsdp")
    z = rep // CROSS
    x = rep % CROSS // CORES
    core = rep % CORES
    chips = CROSS // CORES
    z_peers = [(lax.rem(z + d, depth), lax.rem(core + e, CORES)) for e in range(CORES) for d in range(depth)][1:]
    z_devices = [(to * CROSS + x * CORES + side, me) for to, side in z_peers]
    x_devices = [(z * CROSS + lax.rem(x + d, chips) * CORES + core, me) for d in range(1, chips)]
    other_core = (rep + 1 - 2 * core, me)

    distances = [4, 3, -3, 2, -2, 1, -1, 0]
    last = n_ring - 1
    holder = [lax.rem(me + d + n_ring, n_ring) for d in distances]
    ring = [holder[distances.index(1)], holder[distances.index(-1)]]

    chunk_loads = {}
    for slot, distance in enumerate(distances):
        columns = pl.ds(pl.multiple_of(holder[slot] * width, LANES), width)
        chunk_loads[distance] = pltpu.make_async_copy(
            grads_hbm.at[:, columns], grads.at[slot], chunk_sem.at[slot]
        )
    loads = [
        pltpu.make_async_copy(source, target, load_sem.at[slot])
        for slot, (source, target) in enumerate(
            [
                (indices_hbm, indices), (pair_hbm, pair), (rows_hbm, rows), (momentum_hbm, momentum),
            ]
        )
    ]
    chunk_loads[4].start()
    loads[0].start()
    for distance in distances[1:]:
        chunk_loads[distance].start()
    for load in loads[1:]:
        load.start()

    barrier = pltpu.get_barrier_semaphore()
    for neighbour in holder[:last]:
        pl.semaphore_signal(barrier, inc=1, device_id=(rep, neighbour), device_id_type=MESH)
    for device in z_devices + x_devices:
        pl.semaphore_signal(barrier, inc=1, device_id=device, device_id_type=MESH)

    def own_part(distance, piece, rows=slice(None)):
        slot = distances.index(distance)
        return grads[slot, rows, piece * LANES : (piece + 1) * LANES].astype(jnp.float32)

    def hop(way, step, piece):
        if step == 1:
            rows = pl.ds(0, half) if way == 0 else pl.ds(half, half)
            source = first.at[piece, rows]
            target = partial.at[way, 0, piece, rows]
        else:
            source = partial.at[way, step - 2, piece]
            target = partial.at[way, step - 1, piece]
        return pltpu.make_async_remote_copy(
            src_ref=source,
            dst_ref=target,
            send_sem=send_sem.at[way, step - 1, piece],
            recv_sem=recv_sem.at[way, step - 1, piece],
            device_id=(rep, ring[way]),
            device_id_type=MESH,
        )

    waited = set()

    def need(distance):
        if distance not in waited:
            chunk_loads[distance].wait()
            waited.add(distance)

    need(4)
    for piece in range(pieces):
        first[piece] = own_part(4, piece)
    pl.semaphore_wait(barrier, last + len(z_devices) + len(x_devices))

    def send_first(piece):
        for way in range(2):
            hop(way, 1, piece).start()

    def fill_half(piece):
        need(3)
        need(-3)
        partial[0, 0, piece, half:] = own_part(3, piece, slice(half, None))
        partial[1, 0, piece, :half] = own_part(-3, piece, slice(0, half))

    def send_on(step, piece):
        for way in range(2):
            distance = (5 - step) * (1 if way == 0 else -1)
            need(distance)
            hop(way, step - 1, piece).wait_recv()
            if step == 2:
                rows = slice(0, half) if way == 0 else slice(half, None)
            else:
                rows = slice(None)
            partial[way, step - 2, piece, rows] += own_part(distance, piece, rows)
            hop(way, step, piece).start()

    offset_axis = lax.broadcasted_iota(jnp.int32, (LANES, LANES), 0)
    column_axis = lax.broadcasted_iota(jnp.int32, (LANES, LANES), 0) % SPAN
    low = lax.broadcasted_iota(jnp.int32, (1, LANES), 1) < SPAN
    low_tile = lax.broadcasted_iota(jnp.int32, (SPAN, LANES), 1) < SPAN

    def prepare(piece):
        if piece == 0:
            loads[0].wait()
        parts = [indices[a, 2 * piece + c] for c in range(2) for a in range(2)]
        positions = jnp.concatenate(parts, axis=0)
        offsets[piece, :n_rep] = jnp.transpose(positions & (SPACING - 1))
        line = offsets[piece, pl.ds(rep, 1)]
        turned = pltpu.roll(line, SPAN, 1)
        chosen_at[me, piece, 0] = jnp.where(low, line, turned - SPAN)
        chosen_at[me, piece, 1] = jnp.where(low, turned, line - SPAN)

    def split_tables(_):
        for load in loads[1:]:
            load.wait()
        table = pair[...]
        pair_b[...] = jnp.concatenate(halves(table), axis=1)
        pair_f[...] = split_table(table, 1)
        pair_i[...] = split_table(table, 0)
        high, rest = halves(rows[...])
        rows_f[:LANES] = jnp.concatenate([high, rest], axis=1)
        rows_f[LANES:] = jnp.concatenate([high, jnp.zeros_like(rest)], axis=1)
        rows_i[...] = jnp.concatenate([high, high, rest], axis=1)

    def exchange(ref, sem, slot, row):
        source, target = row
        return pltpu.make_async_remote_copy(
            src_ref=ref[0].at[source],
            dst_ref=ref[1].at[target],
            send_sem=sem.at[0],
            recv_sem=sem.at[1],
            device_id=(rep, holder[slot]),
            device_id_type=MESH,
        )

    def wait_rows(ref, sem):
        rows = ref.at[pl.ds(0, last)]
        pltpu.make_async_copy(rows, rows, sem).wait()

    def send_indices(_):
        for slot in range(last):
            exchange((chosen_at, chosen_at), index_sem, slot, (me, me)).start()

    def along_rows(lines):
        both = dot_nn(jnp.concatenate(halves(lines), axis=1), rows_f[...])
        return both[:, :LANES] + both[:, LANES:]

    def forward(value):
        return along_rows(dot_nt(pair_f[...], split_value(value, 1)))

    def transform(slot):
        need(distances[slot])
        if slot == last:
            for piece in range(pieces):
                columns = slice(piece * LANES, (piece + 1) * LANES)
                spectra[slot, piece] = forward(DECAY * momentum[:, columns] + own_part(0, piece))
            return
        lines = []
        for piece in range(0, pieces, 2):
            parts = [grads[slot, :, q * LANES : (q + 1) * LANES] for q in (piece, piece + 1)]
            parts = jnp.concatenate(parts, axis=0)
            step = dot_nt(pair_b[...], jnp.concatenate([parts, parts], axis=1))
            lines += [step[:, :LANES], step[:, LANES:]]
        spectra[slot] = along_rows(jnp.concatenate(lines, axis=0)).reshape(pieces, LANES, LANES)

    def pick(slot, piece, values):
        at = chosen_at[holder[slot], piece]
        both = jnp.concatenate([jnp.broadcast_to(at[c], (SPAN, LANES)) for c in range(2)], axis=0)
        return jnp.where(column_axis == both, values, 0.0)

    def choose(_):
        wait_rows(chosen_at, index_sem.at[1])
        for slot in range(n_ring):
            for piece in range(pieces):
                chosen = pick(slot, piece, spectra[slot, piece])
                sums = [jnp.sum(chosen[c * SPAN : (c + 1) * SPAN], axis=0, keepdims=True) for c in range(2)]
                sums = [line + pltpu.roll(line, SPAN, 1) for line in sums]
                kept_part[slot, piece] = jnp.where(low, sums[0], sums[1])
            if slot < last:
                exchange((kept_part, kept_in), part_sem, slot, (slot, slot)).start()

    def gather_z(side, device):
        return pltpu.make_async_remote_copy(
            src_ref=kept_own.at[side],
            dst_ref=kept_all.at[:, x, z * CORES + core],
            send_sem=z_send,
            recv_sem=z_recv,
            device_id=device,
            device_id_type=MESH,
        )

    def gather_x(piece, device):
        rows = kept_all.at[piece, x]
        return pltpu.make_async_remote_copy(
            src_ref=rows,
            dst_ref=rows,
            send_sem=x_send.at[piece],
            recv_sem=x_recv.at[piece],
            device_id=device,
            device_id_type=MESH,
        )

    def wait_z(sem):
        rows = kept_all.at[:, 0, pl.ds(0, len(z_devices))]
        pltpu.make_async_copy(rows, rows, sem).wait()

    def wait_x(piece, sem):
        rows = kept_all.at[piece, pl.ds(0, chips - 1)]
        pltpu.make_async_copy(rows, rows, sem.at[piece]).wait()

    def swap(piece):
        start = pl.multiple_of((core * group + piece) * LANES, LANES)
        columns = update.at[:, pl.ds(start, LANES)]
        return pltpu.make_async_remote_copy(
            src_ref=columns,
            dst_ref=columns,
            send_sem=update_send.at[piece],
            recv_sem=update_recv.at[piece],
            device_id=other_core,
            device_id_type=MESH,
        )

    def sum_kept(_):
        wait_rows(kept_in, part_sem.at[1])
        for piece in range(pieces):
            total = kept_part[last, piece]
            for slot in range(last):
                total = total + kept_in[slot, piece]
            kept_own[piece // group, piece % group] = total
        for (_, side), device in zip(z_peers, z_devices):
            gather_z(side, device).start()
        for piece in range(group):
            kept_all[piece, x, z * CORES + core] = kept_own[core, piece]

    def pass_on(_):
        wait_z(z_recv)
        for piece in range(group):
            for device in x_devices:
                gather_x(piece, device).start()

    def inverse(wanted):
        half_way = dot_nt(rows_i[...], split_value(wanted, 1))
        return dot_nn(split_value(half_way, 1), pair_i[...])

    def place(piece):
        wait_x(piece, x_recv)
        piece_at = core * group + piece

        def add_rows(row, total):
            base = pl.multiple_of(row * CROSS, CROSS)
            for member in range(CROSS):
                position = offsets[piece_at, pl.ds(base, CROSS)][member : member + 1]
                value = kept_all[piece, member // CORES, row * CORES + member % CORES]
                total = total + jnp.where(offset_axis == position, value, 0.0)
            return total

        total = lax.fori_loop(0, depth, add_rows, jnp.zeros((LANES, LANES), jnp.float32))
        top, bottom = total[:SPAN], total[SPAN:]
        swapped = [
            jnp.where(low_tile, top, pltpu.roll(bottom, SPAN, 1)),
            jnp.where(low_tile, pltpu.roll(top, SPAN, 1), bottom),
        ]
        columns = pl.ds(pl.multiple_of(piece_at * LANES, LANES), LANES)
        update[:, columns] = inverse(jnp.concatenate(swapped, axis=0))
        swap(piece).start()

    def finish(piece):
        for way in range(2):
            hop(way, 4, piece).wait_recv()
        columns = slice(piece * LANES, (piece + 1) * LANES)
        gradient = own_part(0, piece) + partial[0, 3, piece] + partial[1, 3, piece]
        value = DECAY * momentum[:, columns] + gradient
        remaining[:, columns] = value - inverse(pick(last, piece, forward(value)))

    stages = {
        "first": send_first, "fill": fill_half, "prepare": prepare, "tables": split_tables,
        "indices": send_indices, "transform": transform, "choose": choose, "sum": sum_kept,
        "pass": pass_on, "place": place, "finish": finish,
    }
    for stage, piece in schedule:
        if isinstance(stage, int):
            send_on(stage, piece)
        else:
            stages[stage](piece)

    for piece in range(pieces):
        for way in range(2):
            for step in range(1, 5):
                hop(way, step, piece).wait_send()
    wait_rows(chosen_at, index_sem.at[0])
    wait_rows(kept_part, part_sem.at[0])
    wait_z(z_send)
    for piece in range(group):
        wait_x(piece, x_send)
        swap(piece).wait()


def order():
    def on(step, *which):
        return [(step, p) for p in which]

    return (
        on("first", 0, 1, 2) + on("prepare", 0, 1, 2, 3, 4, 5) + [("indices", 0)] + on("first", 3, 4, 5)
        + on("fill", 0, 1, 2, 3, 4, 5)
        + [("tables", 0)] + on("transform", 0, 1) + on(2, 0, 1) + on("transform", 2, 3) + on(2, 2, 3)
        + on("transform", 4, 5) + on(2, 4, 5) + on("transform", 6, 7)
        + [("choose", 0)] + on(3, 0, 1, 2, 3) + [("sum", 0)] + on(3, 4, 5) + on(4, 0, 1)
        + [("pass", 0)] + on(4, 2, 3)
        + on("place", 0) + on(4, 4) + on("place", 1) + on(4, 5) + on("place", 2)
        + on("finish", 0, 1, 2, 3, 4, 5)
    )


def solution(mesh):
    n_rep, n_ring = mesh.shape["rep"], mesh.shape["fsdp"]
    consts = tables()

    def shards(grads, momentum, indices):
        rows, total_width = grads.shape[2:]
        width = momentum.shape[2]
        pieces = width // LANES
        positions = jnp.transpose(indices, (1, 2, 3, 0))
        grads2, momentum2 = grads.reshape(rows, total_width), momentum.reshape(rows, width)
        f32, bf16 = jnp.float32, jnp.bfloat16
        tile = (LANES, LANES)
        dma = pltpu.SemaphoreType.DMA
        remaining, update = pl.pallas_call(
            functools.partial(kernel, n_rep, n_ring, pieces, order()),
            out_shape=[pltpu.VMEM((rows, width), f32)] * 2,
            in_specs=[pl.BlockSpec(memory_space=pl.ANY)] * 5,
            out_specs=[pl.BlockSpec(memory_space=pltpu.VMEM)] * 2,
            scratch_shapes=[
                pltpu.VMEM((n_ring, rows, width), bf16),
                pltpu.VMEM((rows, width), f32),
                pltpu.VMEM(positions.shape, jnp.int32),
                *[pltpu.VMEM(c.shape, f32) for c in consts],
                pltpu.VMEM((LANES, 2 * LANES), bf16),
                pltpu.VMEM((LANES, 3 * LANES), bf16),
                pltpu.VMEM((2 * LANES, 2 * LANES), bf16),
                pltpu.VMEM((LANES, 3 * LANES), bf16),
                pltpu.VMEM((3 * LANES, LANES), bf16),
                pltpu.VMEM((pieces, *tile), f32),
                pltpu.VMEM((2, 4, pieces, *tile), f32),
                pltpu.VMEM((pieces, *tile), jnp.int32),
                pltpu.VMEM((n_ring, pieces, 2, 1, LANES), jnp.int32),
                pltpu.VMEM((n_ring, pieces, *tile), f32),
                pltpu.VMEM((n_ring, pieces, 1, LANES), f32),
                pltpu.VMEM((n_ring, pieces, 1, LANES), f32),
                pltpu.VMEM((CORES, pieces // CORES, 1, LANES), f32),
                pltpu.VMEM((pieces // CORES, CROSS // CORES, n_rep // CROSS * CORES, 1, LANES), f32),
                dma((4,)),
                dma((n_ring,)),
                dma((2, 4, pieces)),
                dma((2, 4, pieces)),
                dma((2,)),
                dma((2,)),
                dma(()),
                dma(()),
                *[dma((pieces // CORES,))] * 4,
            ],
            compiler_params=pltpu.CompilerParams(
                collective_id=0, has_side_effects=True, vmem_limit_bytes=58 * 2**20
            ),
        )(grads2, momentum2, positions, *[jnp.asarray(c) for c in consts])
        return remaining[None], update

    in_specs = (P("rep", "fsdp", None, None), P("rep", None, "fsdp"), P(None, None, "fsdp", None))
    out_specs = (P("rep", None, "fsdp"), P(None, "fsdp"))
    return jax.shard_map(shards, mesh=mesh, in_specs=in_specs, out_specs=out_specs, check_vma=False)
```

```python
import functools

import jax
import jax.numpy as jnp
import numpy as np
from jax import lax
from jax.experimental import pallas as pl
from jax.experimental.pallas import tpu as pltpu
from jax.sharding import PartitionSpec as P

SPAN = 64
KEEP = 32
LANES = 128
SPACING = SPAN * SPAN // KEEP
CORES = 2
CROSS = 8
DECAY = 0.999
MESH = pl.DeviceIdType.MESH


def tables():
    freq = np.arange(SPAN)[:, None]
    sample = np.arange(SPAN)[None, :]
    c = np.cos(np.pi * (2.0 * sample + 1.0) * freq / (2.0 * SPAN))
    c = c * np.where(freq == 0, np.sqrt(1.0 / SPAN), np.sqrt(2.0 / SPAN))
    pair = np.kron(np.eye(2), c)
    rows = np.concatenate([np.kron(np.eye(2), c[i1::2].T) for i1 in range(2)], axis=1)
    return [t.astype(np.float32) for t in (pair, rows)]


def halves(value):
    high = value.astype(jnp.bfloat16)
    return high, (value - high.astype(jnp.float32)).astype(jnp.bfloat16)


def split_table(table, axis):
    high, low = halves(table)
    return jnp.concatenate([high, high, low], axis=axis)


def split_value(value, axis):
    high, low = halves(value)
    return jnp.concatenate([high, low, high], axis=axis)


def dot_nn(a, b):
    return lax.dot_general(a, b, (((1,), (0,)), ((), ())), preferred_element_type=jnp.float32)


def dot_nt(a, b):
    return lax.dot_general(a, b, (((1,), (1,)), ((), ())), preferred_element_type=jnp.float32)


def kernel(
    n_rep, n_ring, pieces, schedule,
    grads_hbm, momentum_hbm, indices_hbm, pair_hbm, rows_hbm,
    remaining, update,
    grads, momentum, indices, pair, rows, pair_b, pair_f, rows_f, rows_i, pair_i,
    first, partial, offsets, chosen_at, spectra, kept_part, kept_in, kept_own, kept_all,
    load_sem, chunk_sem, send_sem, recv_sem, index_sem, part_sem, z_send, z_recv, x_send, x_recv, update_send, update_recv,
):
    width = pieces * LANES
    depth = n_rep // CROSS
    half = SPAN
    group = pieces // CORES
    rep = lax.axis_index("rep")
    me = lax.axis_index("fsdp")
    z = rep // CROSS
    x = rep % CROSS // CORES
    core = rep % CORES
    chips = CROSS // CORES
    z_peers = [(lax.rem(z + d, depth), lax.rem(core + e, CORES)) for e in range(CORES) for d in range(depth)][1:]
    z_devices = [(to * CROSS + x * CORES + side, me) for to, side in z_peers]
    x_devices = [(z * CROSS + lax.rem(x + d, chips) * CORES + core, me) for d in range(1, chips)]
    other_core = (rep + 1 - 2 * core, me)

    distances = [4, 3, -3, 2, -2, 1, -1, 0]
    last = n_ring - 1
    holder = [lax.rem(me + d + n_ring, n_ring) for d in distances]
    ring = [holder[distances.index(1)], holder[distances.index(-1)]]

    chunk_loads = {}
    for slot, distance in enumerate(distances):
        columns = pl.ds(pl.multiple_of(holder[slot] * width, LANES), width)
        chunk_loads[distance] = pltpu.make_async_copy(
            grads_hbm.at[:, columns], grads.at[slot], chunk_sem.at[slot]
        )
    loads = [
        pltpu.make_async_copy(source, target, load_sem.at[slot])
        for slot, (source, target) in enumerate(
            [
                (indices_hbm, indices), (pair_hbm, pair), (rows_hbm, rows), (momentum_hbm, momentum),
            ]
        )
    ]
    chunk_loads[4].start()
    loads[0].start()
    for distance in distances[1:]:
        chunk_loads[distance].start()
    for load in loads[1:]:
        load.start()

    barrier = pltpu.get_barrier_semaphore()
    for neighbour in holder[:last]:
        pl.semaphore_signal(barrier, inc=1, device_id=(rep, neighbour), device_id_type=MESH)
    for device in z_devices + x_devices:
        pl.semaphore_signal(barrier, inc=1, device_id=device, device_id_type=MESH)

    def own_part(distance, piece, rows=slice(None)):
        slot = distances.index(distance)
        return grads[slot, rows, piece * LANES : (piece + 1) * LANES].astype(jnp.float32)

    def hop(way, step, piece):
        if step == 1:
            rows = pl.ds(0, half) if way == 0 else pl.ds(half, half)
            source = first.at[piece, rows]
            target = partial.at[way, 0, piece, rows]
        else:
            source = partial.at[way, step - 2, piece]
            target = partial.at[way, step - 1, piece]
        return pltpu.make_async_remote_copy(
            src_ref=source,
            dst_ref=target,
            send_sem=send_sem.at[way, step - 1, piece],
            recv_sem=recv_sem.at[way, step - 1, piece],
            device_id=(rep, ring[way]),
            device_id_type=MESH,
        )

    waited = set()

    def need(distance):
        if distance not in waited:
            chunk_loads[distance].wait()
            waited.add(distance)

    def enter(_):
        need(4)
        for piece in range(pieces):
            first[piece] = own_part(4, piece)
        pl.semaphore_wait(barrier, last + len(z_devices) + len(x_devices))

    def send_first(piece):
        for way in range(2):
            hop(way, 1, piece).start()

    def fill_half(piece):
        need(3)
        need(-3)
        partial[0, 0, piece, half:] = own_part(3, piece, slice(half, None))
        partial[1, 0, piece, :half] = own_part(-3, piece, slice(0, half))

    def send_on(step, piece):
        for way in range(2):
            distance = (5 - step) * (1 if way == 0 else -1)
            need(distance)
            hop(way, step - 1, piece).wait_recv()
            if step == 2:
                rows = slice(0, half) if way == 0 else slice(half, None)
            else:
                rows = slice(None)
            partial[way, step - 2, piece, rows] += own_part(distance, piece, rows)
            hop(way, step, piece).start()

    offset_axis = lax.broadcasted_iota(jnp.int32, (LANES, LANES), 0)
    column_axis = lax.broadcasted_iota(jnp.int32, (LANES, LANES), 0) % SPAN
    low = lax.broadcasted_iota(jnp.int32, (1, LANES), 1) < SPAN
    low_tile = lax.broadcasted_iota(jnp.int32, (SPAN, LANES), 1) < SPAN

    def prepare(piece):
        if piece == 0:
            loads[0].wait()
        parts = [indices[a, 2 * piece + c] for c in range(2) for a in range(2)]
        positions = jnp.concatenate(parts, axis=0)
        offsets[piece, :n_rep] = jnp.transpose(positions & (SPACING - 1))
        chosen_at[me, piece] = offsets[piece, pl.ds(rep, 1)]

    def split_tables(_):
        for load in loads[1:]:
            load.wait()
        table = pair[...]
        pair_b[...] = jnp.concatenate(halves(table), axis=1)
        pair_f[...] = split_table(table, 1)
        pair_i[...] = split_table(table, 0)
        high, rest = halves(rows[...])
        rows_f[:LANES] = jnp.concatenate([high, rest], axis=1)
        rows_f[LANES:] = jnp.concatenate([high, jnp.zeros_like(rest)], axis=1)
        rows_i[...] = jnp.concatenate([high, high, rest], axis=1)

    def exchange(ref, sem, slot, row):
        source, target = row
        return pltpu.make_async_remote_copy(
            src_ref=ref[0].at[source],
            dst_ref=ref[1].at[target],
            send_sem=sem.at[0],
            recv_sem=sem.at[1],
            device_id=(rep, holder[slot]),
            device_id_type=MESH,
        )

    def wait_rows(ref, sem):
        rows = ref.at[pl.ds(0, last)]
        pltpu.make_async_copy(rows, rows, sem).wait()

    def send_indices(_):
        for slot in range(last):
            exchange((chosen_at, chosen_at), index_sem, slot, (me, me)).start()

    def along_rows(lines):
        both = dot_nn(jnp.concatenate(halves(lines), axis=1), rows_f[...])
        return both[:, :LANES] + both[:, LANES:]

    def forward(value):
        return along_rows(dot_nt(pair_f[...], split_value(value, 1)))

    def transform(slot):
        need(distances[slot])
        lines = []
        for piece in range(0, pieces, 2):
            parts = [grads[slot, :, q * LANES : (q + 1) * LANES] for q in (piece, piece + 1)]
            parts = jnp.concatenate(parts, axis=0)
            if slot == last:
                old = [momentum[:, q * LANES : (q + 1) * LANES] for q in (piece, piece + 1)]
                value = DECAY * jnp.concatenate(old, axis=0) + parts.astype(jnp.float32)
                step = dot_nt(pair_f[...], split_value(value, 1))
            else:
                step = dot_nt(pair_b[...], jnp.concatenate([parts, parts], axis=1))
            lines += [step[:, :LANES], step[:, LANES:]]
        spectra[slot] = along_rows(jnp.concatenate(lines, axis=0)).reshape(pieces, LANES, LANES)

    def pick(slot, piece, values):
        line = chosen_at[holder[slot], piece]
        turned = pltpu.roll(line, SPAN, 1)
        at = [jnp.where(low, line, turned - SPAN), jnp.where(low, turned, line - SPAN)]
        both = jnp.concatenate([jnp.broadcast_to(row, (SPAN, LANES)) for row in at], axis=0)
        return jnp.where(column_axis == both, values, 0.0)

    def choose(_):
        wait_rows(chosen_at, index_sem.at[1])
        for slot in range(n_ring):
            for piece in range(pieces):
                chosen = pick(slot, piece, spectra[slot, piece])
                sums = [jnp.sum(chosen[c * SPAN : (c + 1) * SPAN], axis=0, keepdims=True) for c in range(2)]
                sums = [line + pltpu.roll(line, SPAN, 1) for line in sums]
                kept_part[slot, piece] = jnp.where(low, sums[0], sums[1])
            if slot < last:
                exchange((kept_part, kept_in), part_sem, slot, (slot, slot)).start()

    def gather_z(side, device):
        return pltpu.make_async_remote_copy(
            src_ref=kept_own.at[side],
            dst_ref=kept_all.at[:, x, z * CORES + core],
            send_sem=z_send,
            recv_sem=z_recv,
            device_id=device,
            device_id_type=MESH,
        )

    def gather_x(piece, device):
        rows = kept_all.at[piece, x]
        return pltpu.make_async_remote_copy(
            src_ref=rows,
            dst_ref=rows,
            send_sem=x_send.at[piece],
            recv_sem=x_recv.at[piece],
            device_id=device,
            device_id_type=MESH,
        )

    def wait_z(sem):
        rows = kept_all.at[:, 0, pl.ds(0, len(z_devices))]
        pltpu.make_async_copy(rows, rows, sem).wait()

    def wait_x(piece, sem):
        rows = kept_all.at[piece, pl.ds(0, chips - 1)]
        pltpu.make_async_copy(rows, rows, sem.at[piece]).wait()

    def swap(piece):
        start = pl.multiple_of((core * group + piece) * LANES, LANES)
        columns = update.at[:, pl.ds(start, LANES)]
        return pltpu.make_async_remote_copy(
            src_ref=columns,
            dst_ref=columns,
            send_sem=update_send.at[piece],
            recv_sem=update_recv.at[piece],
            device_id=other_core,
            device_id_type=MESH,
        )

    def sum_kept(_):
        wait_rows(kept_in, part_sem.at[1])
        for piece in range(pieces):
            total = kept_part[last, piece]
            for slot in range(last):
                total = total + kept_in[slot, piece]
            kept_own[piece // group, piece % group] = total
        for (_, side), device in zip(z_peers, z_devices):
            gather_z(side, device).start()
        for piece in range(group):
            kept_all[piece, x, z * CORES + core] = kept_own[core, piece]

    def pass_on(_):
        wait_z(z_recv)
        for piece in range(group):
            for device in x_devices:
                gather_x(piece, device).start()

    def inverse(wanted):
        half_way = dot_nt(rows_i[...], split_value(wanted, 1))
        return dot_nn(split_value(half_way, 1), pair_i[...])

    def place(piece):
        wait_x(piece, x_recv)
        piece_at = core * group + piece

        def add_rows(row, total):
            base = pl.multiple_of(row * CROSS, CROSS)
            for member in range(CROSS):
                position = offsets[piece_at, pl.ds(base, CROSS)][member : member + 1]
                value = kept_all[piece, member // CORES, row * CORES + member % CORES]
                total = total + jnp.where(offset_axis == position, value, 0.0)
            return total

        total = lax.fori_loop(0, depth, add_rows, jnp.zeros((LANES, LANES), jnp.float32))
        top, bottom = total[:SPAN], total[SPAN:]
        swapped = [
            jnp.where(low_tile, top, pltpu.roll(bottom, SPAN, 1)),
            jnp.where(low_tile, pltpu.roll(top, SPAN, 1), bottom),
        ]
        columns = pl.ds(pl.multiple_of(piece_at * LANES, LANES), LANES)
        update[:, columns] = inverse(jnp.concatenate(swapped, axis=0))
        swap(piece).start()

    def finish(piece):
        for way in range(2):
            hop(way, 4, piece).wait_recv()
        columns = slice(piece * LANES, (piece + 1) * LANES)
        gradient = own_part(0, piece) + partial[0, 3, piece] + partial[1, 3, piece]
        value = DECAY * momentum[:, columns] + gradient
        remaining[:, columns] = value - inverse(pick(last, piece, forward(value)))

    stages = {
        "enter": enter, "first": send_first, "fill": fill_half, "prepare": prepare, "tables": split_tables,
        "indices": send_indices, "transform": transform, "choose": choose, "sum": sum_kept,
        "pass": pass_on, "place": place, "finish": finish,
    }
    for stage, piece in schedule:
        if isinstance(stage, int):
            send_on(stage, piece)
        else:
            stages[stage](piece)

    for piece in range(pieces):
        for way in range(2):
            for step in range(1, 5):
                hop(way, step, piece).wait_send()
    wait_rows(chosen_at, index_sem.at[0])
    wait_rows(kept_part, part_sem.at[0])
    wait_z(z_send)
    for piece in range(group):
        wait_x(piece, x_send)
        swap(piece).wait()


def order():
    def on(step, *which):
        return [(step, p) for p in which]

    return (
        on("prepare", 0, 1, 2, 3, 4, 5) + [("tables", 0), ("enter", 0), ("indices", 0)]
        + on("first", 0, 1, 2, 3, 4, 5) + on("fill", 0, 1, 2, 3, 4, 5)
        + on("transform", 0, 1, 2, 3) + on(2, 0, 1) + on("transform", 4, 5, 6, 7)
        + [("choose", 0)] + on(2, 2, 3, 4, 5) + [("sum", 0)] + on(3, 0, 1, 2, 3, 4, 5)
        + [("pass", 0)] + on(4, 0, 1, 2, 3, 4, 5)
        + on("place", 0, 1, 2) + on("finish", 0, 1, 2, 3, 4, 5)
    )


def solution(mesh):
    n_rep, n_ring = mesh.shape["rep"], mesh.shape["fsdp"]
    consts = tables()

    def shards(grads, momentum, indices):
        rows, total_width = grads.shape[2:]
        width = momentum.shape[2]
        pieces = width // LANES
        positions = jnp.transpose(indices, (1, 2, 3, 0))
        grads2, momentum2 = grads.reshape(rows, total_width), momentum.reshape(rows, width)
        f32, bf16 = jnp.float32, jnp.bfloat16
        tile = (LANES, LANES)
        dma = pltpu.SemaphoreType.DMA
        remaining, update = pl.pallas_call(
            functools.partial(kernel, n_rep, n_ring, pieces, order()),
            out_shape=[pltpu.VMEM((rows, width), f32)] * 2,
            in_specs=[pl.BlockSpec(memory_space=pl.ANY)] * 5,
            out_specs=[pl.BlockSpec(memory_space=pltpu.VMEM)] * 2,
            scratch_shapes=[
                pltpu.VMEM((n_ring, rows, width), bf16),
                pltpu.VMEM((rows, width), f32),
                pltpu.VMEM(positions.shape, jnp.int32),
                *[pltpu.VMEM(c.shape, f32) for c in consts],
                pltpu.VMEM((LANES, 2 * LANES), bf16),
                pltpu.VMEM((LANES, 3 * LANES), bf16),
                pltpu.VMEM((2 * LANES, 2 * LANES), bf16),
                pltpu.VMEM((LANES, 3 * LANES), bf16),
                pltpu.VMEM((3 * LANES, LANES), bf16),
                pltpu.VMEM((pieces, *tile), f32),
                pltpu.VMEM((2, 4, pieces, *tile), f32),
                pltpu.VMEM((pieces, *tile), jnp.int32),
                pltpu.VMEM((n_ring, pieces, 1, LANES), jnp.int32),
                pltpu.VMEM((n_ring, pieces, *tile), f32),
                pltpu.VMEM((n_ring, pieces, 1, LANES), f32),
                pltpu.VMEM((n_ring, pieces, 1, LANES), f32),
                pltpu.VMEM((CORES, pieces // CORES, 1, LANES), f32),
                pltpu.VMEM((pieces // CORES, CROSS // CORES, n_rep // CROSS * CORES, 1, LANES), f32),
                dma((4,)),
                dma((n_ring,)),
                dma((2, 4, pieces)),
                dma((2, 4, pieces)),
                dma((2,)),
                dma((2,)),
                dma(()),
                dma(()),
                *[dma((pieces // CORES,))] * 4,
            ],
            compiler_params=pltpu.CompilerParams(
                collective_id=0, has_side_effects=True, vmem_limit_bytes=58 * 2**20
            ),
        )(grads2, momentum2, positions, *[jnp.asarray(c) for c in consts])
        return remaining[None], update

    in_specs = (P("rep", "fsdp", None, None), P("rep", None, "fsdp"), P(None, None, "fsdp", None))
    out_specs = (P("rep", None, "fsdp"), P(None, "fsdp"))
    return jax.shard_map(shards, mesh=mesh, in_specs=in_specs, out_specs=out_specs, check_vma=False)
```

```python
import functools

import jax
import jax.numpy as jnp
import numpy as np
from jax import lax
from jax.experimental import pallas as pl
from jax.experimental.pallas import tpu as pltpu
from jax.sharding import PartitionSpec as P

SPAN = 64
KEEP = 32
LANES = 128
SPACING = SPAN * SPAN // KEEP
CORES = 2
CROSS = 8
DECAY = 0.999
MESH = pl.DeviceIdType.MESH


def tables():
    freq = np.arange(SPAN)[:, None]
    sample = np.arange(SPAN)[None, :]
    c = np.cos(np.pi * (2.0 * sample + 1.0) * freq / (2.0 * SPAN))
    c = c * np.where(freq == 0, np.sqrt(1.0 / SPAN), np.sqrt(2.0 / SPAN))
    pair = np.kron(np.eye(2), c)
    rows = np.concatenate([np.kron(np.eye(2), c[i1::2].T) for i1 in range(2)], axis=1)
    return [t.astype(np.float32) for t in (pair, rows)]


def halves(value):
    high = value.astype(jnp.bfloat16)
    return high, (value - high.astype(jnp.float32)).astype(jnp.bfloat16)


def split_table(table, axis):
    high, low = halves(table)
    return jnp.concatenate([high, high, low], axis=axis)


def split_value(value, axis):
    high, low = halves(value)
    return jnp.concatenate([high, low, high], axis=axis)


def dot_nn(a, b):
    return lax.dot_general(a, b, (((1,), (0,)), ((), ())), preferred_element_type=jnp.float32)


def dot_nt(a, b):
    return lax.dot_general(a, b, (((1,), (1,)), ((), ())), preferred_element_type=jnp.float32)


def kernel(
    n_rep, n_ring, pieces, schedule,
    grads_hbm, momentum_hbm, indices_hbm, pair_hbm, rows_hbm,
    remaining, update,
    grads, momentum, indices, pair, rows, pair_b, pair_f, rows_f, rows_i, pair_i,
    first, partial, offsets, chosen_at, spectra, kept_part, kept_in, kept_own, kept_all,
    load_sem, chunk_sem, send_sem, recv_sem, index_sem, part_sem, z_send, z_recv, x_send, x_recv, update_send, update_recv, up_sem, ready_sem,
):
    width = pieces * LANES
    depth = n_rep // CROSS
    half = SPAN
    group = pieces // CORES
    rep = lax.axis_index("rep")
    me = lax.axis_index("fsdp")
    z = rep // CROSS
    x = rep % CROSS // CORES
    core = rep % CORES
    chips = CROSS // CORES
    def along_z(to):
        return [(to * CROSS + x * CORES + side, me) for side in range(CORES)]

    above, below = along_z(jnp.minimum(z + 1, depth - 1)), along_z(jnp.maximum(z - 1, 0))
    x_devices = [(z * CROSS + lax.rem(x + d, chips) * CORES + core, me) for d in range(1, chips)]
    other_core = (rep + 1 - 2 * core, me)

    distances = [4, 3, -3, 2, -2, 1, -1, 0]
    last = n_ring - 1
    holder = [lax.rem(me + d + n_ring, n_ring) for d in distances]
    ring = [holder[distances.index(1)], holder[distances.index(-1)]]

    chunk_loads = {}
    for slot, distance in enumerate(distances):
        columns = pl.ds(pl.multiple_of(holder[slot] * width, LANES), width)
        chunk_loads[distance] = pltpu.make_async_copy(
            grads_hbm.at[:, columns], grads.at[slot], chunk_sem.at[slot]
        )
    loads = [
        pltpu.make_async_copy(source, target, load_sem.at[slot])
        for slot, (source, target) in enumerate(
            [
                (indices_hbm, indices), (pair_hbm, pair), (rows_hbm, rows), (momentum_hbm, momentum),
            ]
        )
    ]
    loads[0].start()
    chunk_loads[4].start()
    for load in loads[1:3]:
        load.start()
    for distance in distances[1:]:
        chunk_loads[distance].start()
    loads[3].start()

    barrier = pltpu.get_barrier_semaphore()
    for neighbour in holder[:last]:
        pl.semaphore_signal(barrier, inc=1, device_id=(rep, neighbour), device_id_type=MESH)
    for device in x_devices + [other_core]:
        pl.semaphore_signal(barrier, inc=1, device_id=device, device_id_type=MESH)

    @pl.when(z > 0)
    def _():
        for device in below:
            pl.semaphore_signal(barrier, inc=1, device_id=device, device_id_type=MESH)

    @pl.when(z < depth - 1)
    def _():
        for device in above:
            pl.semaphore_signal(barrier, inc=1, device_id=device, device_id_type=MESH)

    def own_part(distance, piece, rows=slice(None)):
        slot = distances.index(distance)
        return grads[slot, rows, piece * LANES : (piece + 1) * LANES].astype(jnp.float32)

    def hop(way, step, piece):
        if step == 1:
            rows = pl.ds(0, half) if way == 0 else pl.ds(half, half)
            source = first.at[piece, rows]
            target = partial.at[way, 0, piece, rows]
        else:
            source = partial.at[way, step - 2, piece]
            target = partial.at[way, step - 1, piece]
        return pltpu.make_async_remote_copy(
            src_ref=source,
            dst_ref=target,
            send_sem=send_sem.at[way, step - 1, piece],
            recv_sem=recv_sem.at[way, step - 1, piece],
            device_id=(rep, ring[way]),
            device_id_type=MESH,
        )

    waited = set()

    def need(distance):
        if distance not in waited:
            chunk_loads[distance].wait()
            waited.add(distance)

    def enter(_):
        need(4)
        for piece in range(pieces):
            first[piece] = own_part(4, piece)
        neighbours = CORES * (jnp.minimum(z, 1) + jnp.minimum(depth - 1 - z, 1))
        pl.semaphore_wait(barrier, last + len(x_devices) + 1 + neighbours)

    def announce(_):
        @pl.when(z > 0)
        def _():
            pl.semaphore_wait(up_sem, CORES)

        @pl.when(z < depth - 1)
        def _():
            for device in above:
                pl.semaphore_signal(up_sem, inc=1, device_id=device, device_id_type=MESH)

        for step in range(1, depth):

            @pl.when(z >= step)
            def _():
                for device in along_z(z - step):
                    pl.semaphore_signal(ready_sem, inc=1, device_id=device, device_id_type=MESH)


    def send_first(piece):
        for way in range(2):
            hop(way, 1, piece).start()

    def fill_half(piece):
        need(3)
        need(-3)
        partial[0, 0, piece, half:] = own_part(3, piece, slice(half, None))
        partial[1, 0, piece, :half] = own_part(-3, piece, slice(0, half))

    def send_on(step, piece):
        for way in range(2):
            distance = (5 - step) * (1 if way == 0 else -1)
            need(distance)
            hop(way, step - 1, piece).wait_recv()
            if step == 2:
                rows = slice(0, half) if way == 0 else slice(half, None)
            else:
                rows = slice(None)
            partial[way, step - 2, piece, rows] += own_part(distance, piece, rows)
            hop(way, step, piece).start()

    offset_axis = lax.broadcasted_iota(jnp.int32, (LANES, LANES), 0)
    column_axis = lax.broadcasted_iota(jnp.int32, (LANES, LANES), 0) % SPAN
    low = lax.broadcasted_iota(jnp.int32, (1, LANES), 1) < SPAN
    low_tile = lax.broadcasted_iota(jnp.int32, (SPAN, LANES), 1) < SPAN

    def prepare(piece):
        if piece == 0:
            loads[0].wait()
        parts = [indices[a, 2 * piece + c] for c in range(2) for a in range(2)]
        positions = jnp.concatenate(parts, axis=0)
        offsets[piece, :n_rep] = jnp.transpose(positions & (SPACING - 1))
        chosen_at[me, piece] = offsets[piece, pl.ds(rep, 1)]

    def split_tables(_):
        for load in loads[1:]:
            load.wait()
        table = pair[...]
        pair_b[...] = jnp.concatenate(halves(table), axis=1)
        pair_f[...] = split_table(table, 1)
        pair_i[...] = split_table(table, 0)
        high, rest = halves(rows[...])
        rows_f[:LANES] = jnp.concatenate([high, rest], axis=1)
        rows_f[LANES:] = jnp.concatenate([high, jnp.zeros_like(rest)], axis=1)
        rows_i[...] = jnp.concatenate([high, high, rest], axis=1)

    def exchange(ref, sem, slot, row):
        source, target = row
        return pltpu.make_async_remote_copy(
            src_ref=ref[0].at[source],
            dst_ref=ref[1].at[target],
            send_sem=sem.at[0],
            recv_sem=sem.at[1],
            device_id=(rep, holder[slot]),
            device_id_type=MESH,
        )

    def wait_rows(ref, sem):
        rows = ref.at[pl.ds(0, last)]
        pltpu.make_async_copy(rows, rows, sem).wait()

    def send_indices(_):
        for slot in range(last):
            exchange((chosen_at, chosen_at), index_sem, slot, (me, me)).start()

    def along_rows(lines):
        both = dot_nn(jnp.concatenate(halves(lines), axis=1), rows_f[...])
        return both[:, :LANES] + both[:, LANES:]

    def forward(value):
        return along_rows(dot_nt(pair_f[...], split_value(value, 1)))

    def transform(slot):
        need(distances[slot])
        lines = []
        for piece in range(0, pieces, 2):
            parts = [grads[slot, :, q * LANES : (q + 1) * LANES] for q in (piece, piece + 1)]
            parts = jnp.concatenate(parts, axis=0)
            if slot == last:
                old = [momentum[:, q * LANES : (q + 1) * LANES] for q in (piece, piece + 1)]
                value = DECAY * jnp.concatenate(old, axis=0) + parts.astype(jnp.float32)
                step = dot_nt(pair_f[...], split_value(value, 1))
            else:
                step = dot_nt(pair_b[...], jnp.concatenate([parts, parts], axis=1))
            lines += [step[:, :LANES], step[:, LANES:]]
        spectra[slot] = along_rows(jnp.concatenate(lines, axis=0)).reshape(pieces, LANES, LANES)

    def pick(slot, piece, values):
        line = chosen_at[holder[slot], piece]
        turned = pltpu.roll(line, SPAN, 1)
        at = [jnp.where(low, line, turned - SPAN), jnp.where(low, turned, line - SPAN)]
        both = jnp.concatenate([jnp.broadcast_to(row, (SPAN, LANES)) for row in at], axis=0)
        return jnp.where(column_axis == both, values, 0.0)

    def choose(_):
        wait_rows(chosen_at, index_sem.at[1])
        for slot in range(n_ring):
            for piece in range(pieces):
                chosen = pick(slot, piece, spectra[slot, piece])
                sums = [jnp.sum(chosen[c * SPAN : (c + 1) * SPAN], axis=0, keepdims=True) for c in range(2)]
                sums = [line + pltpu.roll(line, SPAN, 1) for line in sums]
                kept_part[slot, piece] = jnp.where(low, sums[0], sums[1])
            if slot < last:
                exchange((kept_part, kept_in), part_sem, slot, (slot, slot)).start()

    def gather_z(side, device):
        return pltpu.make_async_remote_copy(
            src_ref=kept_own.at[side],
            dst_ref=kept_all.at[:, x, z * CORES + core],
            send_sem=z_send,
            recv_sem=z_recv,
            device_id=device,
            device_id_type=MESH,
        )

    def gather_x(piece, device):
        rows = kept_all.at[piece, x]
        return pltpu.make_async_remote_copy(
            src_ref=rows,
            dst_ref=rows,
            send_sem=x_send.at[piece],
            recv_sem=x_recv.at[piece],
            device_id=device,
            device_id_type=MESH,
        )

    def wait_z(sem):
        rows = kept_all.at[:, 0, pl.ds(0, CORES * depth - 1)]
        pltpu.make_async_copy(rows, rows, sem).wait()

    def wait_x(piece, sem):
        rows = kept_all.at[piece, pl.ds(0, chips - 1)]
        pltpu.make_async_copy(rows, rows, sem.at[piece]).wait()

    def swap(piece):
        start = pl.multiple_of((core * group + piece) * LANES, LANES)
        columns = update.at[:, pl.ds(start, LANES)]
        return pltpu.make_async_remote_copy(
            src_ref=columns,
            dst_ref=columns,
            send_sem=update_send.at[piece],
            recv_sem=update_recv.at[piece],
            device_id=other_core,
            device_id_type=MESH,
        )

    def sum_kept(_):
        wait_rows(kept_in, part_sem.at[1])
        for piece in range(pieces):
            total = kept_part[last, piece]
            for slot in range(last):
                total = total + kept_in[slot, piece]
            kept_own[piece // group, piece % group] = total
        for step in range(1, depth):

            @pl.when(z >= step)
            def _():
                for side, device in enumerate(along_z(z - step)):
                    gather_z(side, device).start()

        gather_z(1 - core, other_core).start()
        for piece in range(group):
            kept_all[piece, x, z * CORES + core] = kept_own[core, piece]

    def send_up(_):
        @pl.when(z < depth - 1)
        def _():
            pl.semaphore_wait(ready_sem, CORES * (depth - 1 - z))

        for step in range(1, depth):

            @pl.when(z + step < depth)
            def _():
                for side, device in enumerate(along_z(z + step)):
                    gather_z(side, device).start()

    def pass_on(_):
        wait_z(z_recv)
        for piece in range(group):
            for device in x_devices:
                gather_x(piece, device).start()

    def inverse(wanted):
        half_way = dot_nt(rows_i[...], split_value(wanted, 1))
        return dot_nn(split_value(half_way, 1), pair_i[...])

    def place(piece):
        wait_x(piece, x_recv)
        piece_at = core * group + piece

        def add_rows(row, total):
            base = pl.multiple_of(row * CROSS, CROSS)
            for member in range(CROSS):
                position = offsets[piece_at, pl.ds(base, CROSS)][member : member + 1]
                value = kept_all[piece, member // CORES, row * CORES + member % CORES]
                total = total + jnp.where(offset_axis == position, value, 0.0)
            return total

        total = lax.fori_loop(0, depth, add_rows, jnp.zeros((LANES, LANES), jnp.float32))
        top, bottom = total[:SPAN], total[SPAN:]
        swapped = [
            jnp.where(low_tile, top, pltpu.roll(bottom, SPAN, 1)),
            jnp.where(low_tile, pltpu.roll(top, SPAN, 1), bottom),
        ]
        columns = pl.ds(pl.multiple_of(piece_at * LANES, LANES), LANES)
        update[:, columns] = inverse(jnp.concatenate(swapped, axis=0))
        swap(piece).start()

    def finish(piece):
        for way in range(2):
            hop(way, 4, piece).wait_recv()
        columns = slice(piece * LANES, (piece + 1) * LANES)
        gradient = own_part(0, piece) + partial[0, 3, piece] + partial[1, 3, piece]
        value = DECAY * momentum[:, columns] + gradient
        remaining[:, columns] = value - inverse(pick(last, piece, forward(value)))

    stages = {
        "enter": enter, "announce": announce, "up": send_up, "first": send_first, "fill": fill_half, "prepare": prepare, "tables": split_tables,
        "indices": send_indices, "transform": transform, "choose": choose, "sum": sum_kept,
        "pass": pass_on, "place": place, "finish": finish,
    }
    for stage, piece in schedule:
        if isinstance(stage, int):
            send_on(stage, piece)
        else:
            stages[stage](piece)

    for piece in range(pieces):
        for way in range(2):
            for step in range(1, 5):
                hop(way, step, piece).wait_send()
    wait_rows(chosen_at, index_sem.at[0])
    wait_rows(kept_part, part_sem.at[0])
    wait_z(z_send)
    for piece in range(group):
        wait_x(piece, x_send)
        swap(piece).wait()


def order():
    def on(step, *which):
        return [(step, p) for p in which]

    return (
        [("enter", 0)] + on("first", 0, 1, 2) + on("prepare", 0, 1, 2, 3, 4, 5) + [("indices", 0)]
        + on("first", 3, 4, 5) + on("fill", 0, 1, 2, 3, 4, 5)
        + [("tables", 0)] + on("transform", 0, 1) + [("announce", 0)] + on("transform", 2, 3) + on(2, 0, 1)
        + on("transform", 4, 5, 6, 7)
        + [("choose", 0)] + on(2, 2, 3, 4, 5) + [("sum", 0)] + on(3, 0, 1, 2, 3, 4, 5)
        + [("up", 0)] + on(4, 0, 1, 2, 3, 4, 5) + [("pass", 0)]
        + on("finish", 0, 1, 2) + on("place", 0, 1, 2) + on("finish", 3, 4, 5)
    )


def solution(mesh):
    n_rep, n_ring = mesh.shape["rep"], mesh.shape["fsdp"]
    consts = tables()

    def shards(grads, momentum, indices):
        rows, total_width = grads.shape[2:]
        width = momentum.shape[2]
        pieces = width // LANES
        positions = jnp.transpose(indices, (1, 2, 3, 0))
        grads2, momentum2 = grads.reshape(rows, total_width), momentum.reshape(rows, width)
        f32, bf16 = jnp.float32, jnp.bfloat16
        tile = (LANES, LANES)
        dma = pltpu.SemaphoreType.DMA
        remaining, update = pl.pallas_call(
            functools.partial(kernel, n_rep, n_ring, pieces, order()),
            out_shape=[pltpu.VMEM((rows, width), f32)] * 2,
            in_specs=[pl.BlockSpec(memory_space=pl.ANY)] * 5,
            out_specs=[pl.BlockSpec(memory_space=pltpu.VMEM)] * 2,
            scratch_shapes=[
                pltpu.VMEM((n_ring, rows, width), bf16),
                pltpu.VMEM((rows, width), f32),
                pltpu.VMEM(positions.shape, jnp.int32),
                *[pltpu.VMEM(c.shape, f32) for c in consts],
                pltpu.VMEM((LANES, 2 * LANES), bf16),
                pltpu.VMEM((LANES, 3 * LANES), bf16),
                pltpu.VMEM((2 * LANES, 2 * LANES), bf16),
                pltpu.VMEM((LANES, 3 * LANES), bf16),
                pltpu.VMEM((3 * LANES, LANES), bf16),
                pltpu.VMEM((pieces, *tile), f32),
                pltpu.VMEM((2, 4, pieces, *tile), f32),
                pltpu.VMEM((pieces, *tile), jnp.int32),
                pltpu.VMEM((n_ring, pieces, 1, LANES), jnp.int32),
                pltpu.VMEM((n_ring, pieces, *tile), f32),
                pltpu.VMEM((n_ring, pieces, 1, LANES), f32),
                pltpu.VMEM((n_ring, pieces, 1, LANES), f32),
                pltpu.VMEM((CORES, pieces // CORES, 1, LANES), f32),
                pltpu.VMEM((pieces // CORES, CROSS // CORES, n_rep // CROSS * CORES, 1, LANES), f32),
                dma((4,)),
                dma((n_ring,)),
                dma((2, 4, pieces)),
                dma((2, 4, pieces)),
                dma((2,)),
                dma((2,)),
                dma(()),
                dma(()),
                *[dma((pieces // CORES,))] * 4,
                pltpu.SemaphoreType.REGULAR,
                pltpu.SemaphoreType.REGULAR,
            ],
            compiler_params=pltpu.CompilerParams(
                collective_id=0, has_side_effects=True, vmem_limit_bytes=58 * 2**20
            ),
        )(grads2, momentum2, positions, *[jnp.asarray(c) for c in consts])
        return remaining[None], update

    in_specs = (P("rep", "fsdp", None, None), P("rep", None, "fsdp"), P(None, None, "fsdp", None))
    out_specs = (P("rep", None, "fsdp"), P(None, "fsdp"))
    return jax.shard_map(shards, mesh=mesh, in_specs=in_specs, out_specs=out_specs, check_vma=False)
```

```python
import functools

import jax
import jax.numpy as jnp
import numpy as np
from jax import lax
from jax.experimental import pallas as pl
from jax.experimental.pallas import tpu as pltpu
from jax.sharding import PartitionSpec as P

SPAN = 64
KEEP = 32
LANES = 128
SPACING = SPAN * SPAN // KEEP
CORES = 2
CROSS = 8
DECAY = 0.999
MESH = pl.DeviceIdType.MESH


def tables():
    freq = np.arange(SPAN)[:, None]
    sample = np.arange(SPAN)[None, :]
    c = np.cos(np.pi * (2.0 * sample + 1.0) * freq / (2.0 * SPAN))
    c = c * np.where(freq == 0, np.sqrt(1.0 / SPAN), np.sqrt(2.0 / SPAN))
    pair = np.kron(np.eye(2), c)
    rows = np.concatenate([np.kron(np.eye(2), c[i1::2].T) for i1 in range(2)], axis=1)
    return [t.astype(np.float32) for t in (pair, rows)]


def halves(value):
    high = value.astype(jnp.bfloat16)
    return high, (value - high.astype(jnp.float32)).astype(jnp.bfloat16)


def split_table(table, axis):
    high, low = halves(table)
    return jnp.concatenate([high, high, low], axis=axis)


def split_value(value, axis):
    high, low = halves(value)
    return jnp.concatenate([high, low, high], axis=axis)


def dot_nn(a, b):
    return lax.dot_general(a, b, (((1,), (0,)), ((), ())), preferred_element_type=jnp.float32)


def dot_nt(a, b):
    return lax.dot_general(a, b, (((1,), (1,)), ((), ())), preferred_element_type=jnp.float32)


def kernel(
    n_rep, n_ring, pieces, schedule,
    grads_hbm, momentum_hbm, indices_hbm, pair_hbm, rows_hbm,
    remaining, update,
    grads, momentum, indices, pair, rows, pair_b, pair_f, rows_f, rows_i, pair_i,
    first, partial, offsets, chosen_at, spectra, kept_part, kept_in, kept_own, kept_all,
    load_sem, chunk_sem, send_sem, recv_sem, index_sem, part_sem, z_send, z_recv, x_send, x_recv, update_send, update_recv, up_sem, ready_sem,
):
    width = pieces * LANES
    depth = n_rep // CROSS
    half = SPAN
    group = pieces // CORES
    rep = lax.axis_index("rep")
    me = lax.axis_index("fsdp")
    z = rep // CROSS
    x = rep % CROSS // CORES
    core = rep % CORES
    chips = CROSS // CORES
    def along_z(to):
        return [(to * CROSS + x * CORES + side, me) for side in range(CORES)]

    above, below = along_z(jnp.minimum(z + 1, depth - 1)), along_z(jnp.maximum(z - 1, 0))
    x_devices = [(z * CROSS + lax.rem(x + d, chips) * CORES + core, me) for d in range(1, chips)]
    other_core = (rep + 1 - 2 * core, me)

    distances = [4, 3, -3, 2, -2, 1, -1, 0]
    last = n_ring - 1
    holder = [lax.rem(me + d + n_ring, n_ring) for d in distances]
    ring = [holder[distances.index(1)], holder[distances.index(-1)]]

    chunk_loads = {}
    for slot, distance in enumerate(distances):
        columns = pl.ds(pl.multiple_of(holder[slot] * width, LANES), width)
        chunk_loads[distance] = pltpu.make_async_copy(
            grads_hbm.at[:, columns], grads.at[slot], chunk_sem.at[slot]
        )
    loads = [
        pltpu.make_async_copy(source, target, load_sem.at[slot])
        for slot, (source, target) in enumerate(
            [
                (indices_hbm, indices), (pair_hbm, pair), (rows_hbm, rows), (momentum_hbm, momentum),
            ]
        )
    ]
    loads[0].start()
    chunk_loads[4].start()
    for load in loads[1:3]:
        load.start()
    for distance in distances[1:]:
        chunk_loads[distance].start()
    loads[3].start()

    barrier = pltpu.get_barrier_semaphore()
    for neighbour in holder[:last]:
        pl.semaphore_signal(barrier, inc=1, device_id=(rep, neighbour), device_id_type=MESH)
    for device in x_devices + [other_core]:
        pl.semaphore_signal(barrier, inc=1, device_id=device, device_id_type=MESH)

    @pl.when(z > 0)
    def _():
        for device in below:
            pl.semaphore_signal(barrier, inc=1, device_id=device, device_id_type=MESH)

    @pl.when(z < depth - 1)
    def _():
        for device in above:
            pl.semaphore_signal(barrier, inc=1, device_id=device, device_id_type=MESH)

    def own_part(distance, piece, rows=slice(None)):
        slot = distances.index(distance)
        return grads[slot, rows, piece * LANES : (piece + 1) * LANES].astype(jnp.float32)

    def hop(way, step, piece):
        if step == 1:
            rows = pl.ds(0, half) if way == 0 else pl.ds(half, half)
            source = first.at[piece, rows]
            target = partial.at[way, 0, piece, rows]
        else:
            source = partial.at[way, step - 2, piece]
            target = partial.at[way, step - 1, piece]
        return pltpu.make_async_remote_copy(
            src_ref=source,
            dst_ref=target,
            send_sem=send_sem.at[way, step - 1, piece],
            recv_sem=recv_sem.at[way, step - 1, piece],
            device_id=(rep, ring[way]),
            device_id_type=MESH,
        )

    waited = set()

    def need(distance):
        if distance not in waited:
            chunk_loads[distance].wait()
            waited.add(distance)

    def enter(_):
        need(4)
        for piece in range(pieces):
            first[piece] = own_part(4, piece)
        neighbours = CORES * (jnp.minimum(z, 1) + jnp.minimum(depth - 1 - z, 1))
        pl.semaphore_wait(barrier, last + len(x_devices) + 1 + neighbours)

    def announce(_):
        @pl.when(z > 0)
        def _():
            pl.semaphore_wait(up_sem, CORES)

        @pl.when(z < depth - 1)
        def _():
            for device in above:
                pl.semaphore_signal(up_sem, inc=1, device_id=device, device_id_type=MESH)

        for step in range(1, depth):

            @pl.when(z >= step)
            def _():
                for device in along_z(z - step):
                    pl.semaphore_signal(ready_sem, inc=1, device_id=device, device_id_type=MESH)


    def send_first(piece):
        for way in range(2):
            hop(way, 1, piece).start()

    def fill_half(piece):
        need(3)
        need(-3)
        partial[0, 0, piece, half:] = own_part(3, piece, slice(half, None))
        partial[1, 0, piece, :half] = own_part(-3, piece, slice(0, half))

    def send_on(step, piece):
        for way in range(2):
            distance = (5 - step) * (1 if way == 0 else -1)
            need(distance)
            hop(way, step - 1, piece).wait_recv()
            if step == 2:
                rows = slice(0, half) if way == 0 else slice(half, None)
            else:
                rows = slice(None)
            partial[way, step - 2, piece, rows] += own_part(distance, piece, rows)
            hop(way, step, piece).start()

    offset_axis = lax.broadcasted_iota(jnp.int32, (LANES, LANES), 0)
    column_axis = lax.broadcasted_iota(jnp.int32, (LANES, LANES), 0) % SPAN
    low = lax.broadcasted_iota(jnp.int32, (1, LANES), 1) < SPAN
    low_tile = lax.broadcasted_iota(jnp.int32, (SPAN, LANES), 1) < SPAN

    def prepare(piece):
        if piece == 0:
            loads[0].wait()
        parts = [indices[a, 2 * piece + c] for c in range(2) for a in range(2)]
        positions = jnp.concatenate(parts, axis=0)
        offsets[piece, :n_rep] = jnp.transpose(positions & (SPACING - 1))
        chosen_at[me, piece] = offsets[piece, pl.ds(rep, 1)]

    def split_tables(_):
        for load in loads[1:3]:
            load.wait()
        table = pair[...]
        pair_b[...] = jnp.concatenate(halves(table), axis=1)
        pair_f[...] = split_table(table, 1)
        pair_i[...] = split_table(table, 0)
        high, rest = halves(rows[...])
        rows_f[:LANES] = jnp.concatenate([high, rest], axis=1)
        rows_f[LANES:] = jnp.concatenate([high, jnp.zeros_like(rest)], axis=1)
        rows_i[...] = jnp.concatenate([high, high, rest], axis=1)

    def exchange(ref, sem, slot, row):
        source, target = row
        return pltpu.make_async_remote_copy(
            src_ref=ref[0].at[source],
            dst_ref=ref[1].at[target],
            send_sem=sem.at[0],
            recv_sem=sem.at[1],
            device_id=(rep, holder[slot]),
            device_id_type=MESH,
        )

    def wait_rows(ref, sem):
        rows = ref.at[pl.ds(0, last)]
        pltpu.make_async_copy(rows, rows, sem).wait()

    def send_indices(_):
        for slot in range(last):
            exchange((chosen_at, chosen_at), index_sem, slot, (me, me)).start()

    def along_rows(lines):
        both = dot_nn(jnp.concatenate(halves(lines), axis=1), rows_f[...])
        return both[:, :LANES] + both[:, LANES:]

    def forward(value):
        return along_rows(dot_nt(pair_f[...], split_value(value, 1)))

    def transform(slot):
        need(distances[slot])
        if slot == last:
            loads[3].wait()
        lines = []
        for piece in range(0, pieces, 2):
            parts = [grads[slot, :, q * LANES : (q + 1) * LANES] for q in (piece, piece + 1)]
            parts = jnp.concatenate(parts, axis=0)
            if slot == last:
                old = [momentum[:, q * LANES : (q + 1) * LANES] for q in (piece, piece + 1)]
                value = DECAY * jnp.concatenate(old, axis=0) + parts.astype(jnp.float32)
                step = dot_nt(pair_f[...], split_value(value, 1))
            else:
                step = dot_nt(pair_b[...], jnp.concatenate([parts, parts], axis=1))
            lines += [step[:, :LANES], step[:, LANES:]]
        spectra[slot] = along_rows(jnp.concatenate(lines, axis=0)).reshape(pieces, LANES, LANES)

    def pick(slot, piece, values):
        line = chosen_at[holder[slot], piece]
        turned = pltpu.roll(line, SPAN, 1)
        at = [jnp.where(low, line, turned - SPAN), jnp.where(low, turned, line - SPAN)]
        both = jnp.concatenate([jnp.broadcast_to(row, (SPAN, LANES)) for row in at], axis=0)
        return jnp.where(column_axis == both, values, 0.0)

    def choose(_):
        wait_rows(chosen_at, index_sem.at[1])
        for slot in range(n_ring):
            for piece in range(pieces):
                chosen = pick(slot, piece, spectra[slot, piece])
                sums = [jnp.sum(chosen[c * SPAN : (c + 1) * SPAN], axis=0, keepdims=True) for c in range(2)]
                sums = [line + pltpu.roll(line, SPAN, 1) for line in sums]
                kept_part[slot, piece] = jnp.where(low, sums[0], sums[1])
            if slot < last:
                exchange((kept_part, kept_in), part_sem, slot, (slot, slot)).start()

    def gather_z(side, device):
        return pltpu.make_async_remote_copy(
            src_ref=kept_own.at[side],
            dst_ref=kept_all.at[:, x, z * CORES + core],
            send_sem=z_send,
            recv_sem=z_recv,
            device_id=device,
            device_id_type=MESH,
        )

    def gather_x(piece, device):
        rows = kept_all.at[piece, x]
        return pltpu.make_async_remote_copy(
            src_ref=rows,
            dst_ref=rows,
            send_sem=x_send.at[piece],
            recv_sem=x_recv.at[piece],
            device_id=device,
            device_id_type=MESH,
        )

    def wait_z(sem):
        rows = kept_all.at[:, 0, pl.ds(0, CORES * depth - 1)]
        pltpu.make_async_copy(rows, rows, sem).wait()

    def wait_x(piece, sem):
        rows = kept_all.at[piece, pl.ds(0, chips - 1)]
        pltpu.make_async_copy(rows, rows, sem.at[piece]).wait()

    def swap(piece):
        start = pl.multiple_of((core * group + piece) * LANES, LANES)
        columns = update.at[:, pl.ds(start, LANES)]
        return pltpu.make_async_remote_copy(
            src_ref=columns,
            dst_ref=columns,
            send_sem=update_send.at[piece],
            recv_sem=update_recv.at[piece],
            device_id=other_core,
            device_id_type=MESH,
        )

    def sum_kept(_):
        wait_rows(kept_in, part_sem.at[1])
        for piece in range(pieces):
            total = kept_part[last, piece]
            for slot in range(last):
                total = total + kept_in[slot, piece]
            kept_own[piece // group, piece % group] = total
        for step in range(1, depth):

            @pl.when(z >= step)
            def _():
                for side, device in enumerate(along_z(z - step)):
                    gather_z(side, device).start()

        gather_z(1 - core, other_core).start()
        for piece in range(group):
            kept_all[piece, x, z * CORES + core] = kept_own[core, piece]

    def send_up(_):
        @pl.when(z < depth - 1)
        def _():
            pl.semaphore_wait(ready_sem, CORES * (depth - 1 - z))

        for step in range(1, depth):

            @pl.when(z + step < depth)
            def _():
                for side, device in enumerate(along_z(z + step)):
                    gather_z(side, device).start()

    def pass_on(_):
        wait_z(z_recv)
        for piece in range(group):
            for device in x_devices:
                gather_x(piece, device).start()

    def inverse(wanted):
        half_way = dot_nt(rows_i[...], split_value(wanted, 1))
        return dot_nn(split_value(half_way, 1), pair_i[...])

    def place(piece):
        wait_x(piece, x_recv)
        piece_at = core * group + piece

        def add_rows(row, total):
            base = pl.multiple_of(row * CROSS, CROSS)
            for member in range(CROSS):
                position = offsets[piece_at, pl.ds(base, CROSS)][member : member + 1]
                value = kept_all[piece, member // CORES, row * CORES + member % CORES]
                total = total + jnp.where(offset_axis == position, value, 0.0)
            return total

        total = lax.fori_loop(0, depth, add_rows, jnp.zeros((LANES, LANES), jnp.float32))
        top, bottom = total[:SPAN], total[SPAN:]
        swapped = [
            jnp.where(low_tile, top, pltpu.roll(bottom, SPAN, 1)),
            jnp.where(low_tile, pltpu.roll(top, SPAN, 1), bottom),
        ]
        columns = pl.ds(pl.multiple_of(piece_at * LANES, LANES), LANES)
        update[:, columns] = inverse(jnp.concatenate(swapped, axis=0))
        swap(piece).start()

    def finish(piece):
        for way in range(2):
            hop(way, 4, piece).wait_recv()
        columns = slice(piece * LANES, (piece + 1) * LANES)
        gradient = own_part(0, piece) + partial[0, 3, piece] + partial[1, 3, piece]
        value = DECAY * momentum[:, columns] + gradient
        remaining[:, columns] = value - inverse(pick(last, piece, forward(value)))

    stages = {
        "enter": enter, "announce": announce, "up": send_up, "first": send_first, "fill": fill_half, "prepare": prepare, "tables": split_tables,
        "indices": send_indices, "transform": transform, "choose": choose, "sum": sum_kept,
        "pass": pass_on, "place": place, "finish": finish,
    }
    for stage, piece in schedule:
        if isinstance(stage, int):
            send_on(stage, piece)
        else:
            stages[stage](piece)

    for piece in range(pieces):
        for way in range(2):
            for step in range(1, 5):
                hop(way, step, piece).wait_send()
    wait_rows(chosen_at, index_sem.at[0])
    wait_rows(kept_part, part_sem.at[0])
    wait_z(z_send)
    for piece in range(group):
        wait_x(piece, x_send)
        swap(piece).wait()


def order():
    def on(step, *which):
        return [(step, p) for p in which]

    return (
        on("prepare", 0, 1, 2, 3, 4, 5) + [("tables", 0), ("enter", 0), ("indices", 0)]
        + on("first", 0, 1, 2, 3, 4, 5) + on("fill", 0, 1, 2, 3, 4, 5)
        + on("transform", 0, 1) + [("announce", 0)] + on("transform", 2, 3) + on(2, 0, 1)
        + on("transform", 4, 5, 6, 7) + [("choose", 0)] + on(2, 2, 3, 4, 5)
        + [("sum", 0)] + on(3, 0, 1, 2, 3, 4, 5)
        + [("up", 0)] + on(4, 0, 1, 2, 3) + [("pass", 0)] + on(4, 4, 5)
        + on("finish", 0, 1) + on("place", 0, 1, 2) + on("finish", 2, 3, 4, 5)
    )


def solution(mesh):
    n_rep, n_ring = mesh.shape["rep"], mesh.shape["fsdp"]
    consts = tables()

    def shards(grads, momentum, indices):
        rows, total_width = grads.shape[2:]
        width = momentum.shape[2]
        pieces = width // LANES
        positions = jnp.transpose(indices, (1, 2, 3, 0))
        grads2, momentum2 = grads.reshape(rows, total_width), momentum.reshape(rows, width)
        f32, bf16 = jnp.float32, jnp.bfloat16
        tile = (LANES, LANES)
        dma = pltpu.SemaphoreType.DMA
        remaining, update = pl.pallas_call(
            functools.partial(kernel, n_rep, n_ring, pieces, order()),
            out_shape=[pltpu.VMEM((rows, width), f32)] * 2,
            in_specs=[pl.BlockSpec(memory_space=pl.ANY)] * 5,
            out_specs=[pl.BlockSpec(memory_space=pltpu.VMEM)] * 2,
            scratch_shapes=[
                pltpu.VMEM((n_ring, rows, width), bf16),
                pltpu.VMEM((rows, width), f32),
                pltpu.VMEM(positions.shape, jnp.int32),
                *[pltpu.VMEM(c.shape, f32) for c in consts],
                pltpu.VMEM((LANES, 2 * LANES), bf16),
                pltpu.VMEM((LANES, 3 * LANES), bf16),
                pltpu.VMEM((2 * LANES, 2 * LANES), bf16),
                pltpu.VMEM((LANES, 3 * LANES), bf16),
                pltpu.VMEM((3 * LANES, LANES), bf16),
                pltpu.VMEM((pieces, *tile), f32),
                pltpu.VMEM((2, 4, pieces, *tile), f32),
                pltpu.VMEM((pieces, *tile), jnp.int32),
                pltpu.VMEM((n_ring, pieces, 1, LANES), jnp.int32),
                pltpu.VMEM((n_ring, pieces, *tile), f32),
                pltpu.VMEM((n_ring, pieces, 1, LANES), f32),
                pltpu.VMEM((n_ring, pieces, 1, LANES), f32),
                pltpu.VMEM((CORES, pieces // CORES, 1, LANES), f32),
                pltpu.VMEM((pieces // CORES, CROSS // CORES, n_rep // CROSS * CORES, 1, LANES), f32),
                dma((4,)),
                dma((n_ring,)),
                dma((2, 4, pieces)),
                dma((2, 4, pieces)),
                dma((2,)),
                dma((2,)),
                dma(()),
                dma(()),
                *[dma((pieces // CORES,))] * 4,
                pltpu.SemaphoreType.REGULAR,
                pltpu.SemaphoreType.REGULAR,
            ],
            compiler_params=pltpu.CompilerParams(
                collective_id=0, has_side_effects=True, vmem_limit_bytes=58 * 2**20
            ),
        )(grads2, momentum2, positions, *[jnp.asarray(c) for c in consts])

        def copy_out(a, b, c, d, sems):
            one = pltpu.make_async_copy(a, c, sems.at[0])
            two = pltpu.make_async_copy(b, d, sems.at[1])
            one.start()
            two.start()
            one.wait()
            two.wait()

        remaining, update = pl.pallas_call(
            copy_out,
            out_shape=[jax.ShapeDtypeStruct((rows, width), f32)] * 2,
            in_specs=[pl.BlockSpec(memory_space=pltpu.VMEM)] * 2,
            out_specs=[pl.BlockSpec(memory_space=pl.ANY)] * 2,
            scratch_shapes=[dma((2,))],
        )(*[pltpu.with_memory_space_constraint(v, pltpu.VMEM) for v in (remaining, update)])
        return remaining[None], update

    in_specs = (P("rep", "fsdp", None, None), P("rep", None, "fsdp"), P(None, None, "fsdp", None))
    out_specs = (P("rep", None, "fsdp"), P(None, "fsdp"))
    return jax.shard_map(shards, mesh=mesh, in_specs=in_specs, out_specs=out_specs, check_vma=False)
```
